256 devices in a mesh: row: 32 (over x, y, core), col: 8 (over z).
Axes of the slice: x: 4, y: 4, z: 8, core: 2. Of those that a mesh axis runs over, the one named last changes fastest.
Arguments:
- psi: bfloat16 [81920, 64], P('row'), may hold values from -6 to 6
- block_len: int32 [320], P('row'), may hold values from 1 to 256, as said below
- targets: int32 [320, 4], P('row'), may hold values from 0 to 319, as said below
- counts: int32 [320], P('row'), may hold values from 1 to 4, as said below
- dipole: bfloat16 [320, 4, 256, 256], P('row', None, 'col'), may hold values from -0.25 to 0.25
- eigvec: bfloat16 [81920, 8192], P('row', 'col'), may hold values from -0.03125 to 0.03125
Outputs:
- elements: float32 [8192, 64], P('col')
The draws below stay inside these ranges and needn't reach their ends.
Inputs may be any that keep to these rules, and one draw needn't show every extreme that they name: `block_len`: some block has length 256 and some length 1. `targets`: each target lies within 2 blocks of its own block; some lie exactly 2 below and 2 above. `counts`: some block uses all 4 slots.
All inputs are finite; a program needn't handle non-finite values.
Results may differ from the reference program's by a relative error of at most 0.003.
Values may be sent and summed in bfloat16 or wider, within the bound.
A program may use at most 64 MiB of HBM per device.

```python
import jax
import jax.numpy as jnp
from jax import lax

BS = 256
STATES = 64
KMAX = 4
WB = 2
NBLK = 320
ORDER = 81920
SLAB = 8192
SUB = 1
N_ROW = 32
N_COL = 8


def draw_block_len(key, part):
    key = jax.random.fold_in(key, 11)
    key_len, key_long, key_short = jax.random.split(key, 3)
    lengths = jax.random.randint(key_len, (NBLK,), 1, BS + 1)
    longest = jax.random.randint(key_long, (), 0, NBLK)
    shortest = (longest + 1 + jax.random.randint(key_short, (), 0, NBLK - 1)) % NBLK
    lengths = lengths.at[longest].set(BS).at[shortest].set(1)
    return lengths.astype(jnp.int32)


def draw_targets(key, part):
    key = jax.random.fold_in(key, 23)
    offsets = jax.random.randint(key, (NBLK, KMAX), -WB, WB + 1)
    own_block = jnp.arange(NBLK, dtype=jnp.int32)[:, None]
    chosen = jnp.clip(own_block + offsets, 0, NBLK - 1)
    middle = NBLK // 2
    chosen = chosen.at[0, 0].set(0).at[NBLK - 1, 0].set(NBLK - 1)
    chosen = chosen.at[middle, 1].set(middle - WB).at[middle, 2].set(middle + WB)
    return chosen.astype(jnp.int32)


def draw_counts(key, part):
    key = jax.random.fold_in(key, 37)
    key_count, key_full = jax.random.split(key)
    values = jax.random.randint(key_count, (NBLK,), 1, KMAX + 1)
    fullest = jax.random.randint(key_full, (), 0, NBLK)
    return values.at[fullest].set(KMAX).astype(jnp.int32)


def block_scale(rng, extent, cuts, least, top_value):
    level = 1.0
    for axis_at, parts in cuts:
        draws = jax.random.uniform(jax.random.fold_in(jax.random.fold_in(rng, 6), axis_at), (parts,), jnp.float32, least / len(cuts), top_value / len(cuts))
        level = level * jnp.repeat(jnp.exp(draws), extent[axis_at] // parts).reshape((-1,) + (1,) * (len(extent) - 1 - axis_at))
    return level


def normal_values(key, extent, spread, limit, cuts=(), kind=jnp.bfloat16):
    factor_of = block_scale(key, extent, cuts, -0.22, 0.18) if cuts else 1.0
    drawn = jax.random.normal(key, extent, jnp.float32) * spread * factor_of
    return jnp.minimum(jnp.maximum(drawn, -limit), limit).astype(kind)


def setup_inputs(seed: int = 0) -> dict:
    keys = jax.random.split(jax.random.key(seed), 7)
    return {
        "psi": normal_values(keys[0], (ORDER, STATES), 1.0, 6.0, ((0, 32),)),
        "block_len": draw_block_len(jax.random.fold_in(keys[6], 71), 0),
        "targets": draw_targets(jax.random.fold_in(keys[6], 71), 0),
        "counts": draw_counts(jax.random.fold_in(keys[6], 71), 0),
        "dipole": normal_values(keys[4], (NBLK, KMAX, BS, BS), (KMAX * BS // 2) ** -0.5, 0.25, ((0, 32), (2, 8))),
        "eigvec": normal_values(keys[5], (ORDER, SLAB), (ORDER // 2) ** -0.5, 0.03125, ((0, 32), (1, 8))),
    }


def reference(psi, block_len, targets, counts, dipole, eigvec):
    positions = jnp.arange(BS, dtype=jnp.int32)
    row_used = positions[None, :] < block_len[:, None]
    blocks = psi.reshape(NBLK, BS, STATES)
    blocks = jnp.where(row_used[:, :, None], blocks, jnp.zeros((), jnp.bfloat16))
    slot_flags = jnp.arange(KMAX, dtype=jnp.int32)[None, :] < counts[:, None]

    def block_term(items):
        block_tiles, block_targets, block_flags = items
        chosen = blocks[block_targets]
        chosen = jnp.where(block_flags[:, None, None], chosen, jnp.zeros((), jnp.bfloat16))
        return jnp.einsum('krs,ksn->rn', block_tiles.astype(jnp.float32), chosen.astype(jnp.float32))

    product = lax.map(block_term, (dipole, targets, slot_flags))
    product = jnp.where(row_used[:, :, None], product, jnp.float32(0.0)).astype(jnp.bfloat16)
    reordered = product.reshape(NBLK, N_COL, N_ROW, SUB, STATES).transpose(2, 1, 0, 3, 4).reshape(ORDER, STATES)
    return lax.dot_general(eigvec, reordered, (((0,), (0,)), ((), ())), preferred_element_type=jnp.float32)
```

```python
import functools

import jax
import jax.numpy as jnp
from jax import lax
from jax.experimental import pallas as pl
from jax.experimental.pallas import tpu as pltpu
from jax.sharding import PartitionSpec as P

WB = 2
MESH = pl.DeviceIdType.MESH
NT = (((1,), (1,)), ((), ()))
PAD = 16


def body(
    n_row, n_col, nb, kmax, bs, st,
    lens, targets, counts, psi_hbm, dip_hbm, eig_hbm, out_ref,
    psi_v, ext, dip_v, eig_v, stage, msg, recv, gath, acc, rs_recv,
    ld_sem, halo_send, halo_recv, a2a_send, a2a_recv, z_send, z_recv,
    rs_send, rs_sem, ag_send, ag_sem,
):
    row = lax.axis_index("row")
    col = lax.axis_index("col")
    piece = nb * n_row
    f32, bf16 = jnp.float32, jnp.bfloat16

    ld_psi = pltpu.make_async_copy(psi_hbm, psi_v, ld_sem.at[0])
    ld_dip = pltpu.make_async_copy(dip_hbm, dip_v, ld_sem.at[1])
    ld_eig = pltpu.make_async_copy(eig_hbm, eig_v, ld_sem.at[2])
    ld_psi.start()
    ld_dip.start()
    ld_eig.start()

    barrier = pltpu.get_barrier_semaphore()

    def greet_row(i, carry):
        pl.semaphore_signal(
            barrier, inc=1, device_id=(lax.rem(row + i, n_row), col), device_id_type=MESH
        )
        return carry

    def greet_col(i, carry):
        pl.semaphore_signal(
            barrier, inc=1, device_id=(row, lax.rem(col + i, n_col)), device_id_type=MESH
        )
        return carry

    lax.fori_loop(1, n_row, greet_row, 0)
    lax.fori_loop(1, n_col, greet_col, 0)

    stage[...] = jnp.zeros_like(stage)
    ld_psi.wait()
    lane = lax.broadcasted_iota(jnp.int32, (st, bs), 1)
    order = list(range(WB)) + list(range(nb - WB, nb)) + list(range(WB, nb - WB))
    for b in order:
        block = psi_v[:, b * bs : (b + 1) * bs]
        ext[b + WB] = jnp.where(lane < lens[b], block, jnp.zeros((), bf16))

    wanted = lax.broadcasted_iota(jnp.int32, (n_row * PAD, piece), 1)
    wanted = wanted + (PAD - nb) * (wanted // nb)
    have = lax.broadcasted_iota(jnp.int32, (n_row * PAD, piece), 0)
    select = jnp.where(have == wanted, 1.0, 0.0).astype(bf16)

    pl.semaphore_wait(barrier, n_row - 1 + n_col - 1)

    right = lax.rem(row + 1, n_row)
    left = lax.rem(row + n_row - 1, n_row)
    to_right = pltpu.make_async_remote_copy(
        src_ref=ext.at[pl.ds(nb, WB)], dst_ref=ext.at[pl.ds(0, WB)],
        send_sem=halo_send.at[0], recv_sem=halo_recv.at[0],
        device_id=(right, col), device_id_type=MESH,
    )
    to_left = pltpu.make_async_remote_copy(
        src_ref=ext.at[pl.ds(WB, WB)], dst_ref=ext.at[pl.ds(nb + WB, WB)],
        send_sem=halo_send.at[1], recv_sem=halo_recv.at[1],
        device_id=(left, col), device_id_type=MESH,
    )
    to_right.start()
    to_left.start()
    ld_dip.wait()
    to_right.wait()
    to_left.wait()

    first = row * nb - WB
    sub = n_row
    kept = lax.broadcasted_iota(jnp.int32, (sub, st), 0) + col * sub
    for b in range(nb):
        total = jnp.zeros((sub, st), f32)
        for k in range(kmax):
            chosen = ext[jnp.clip(targets[k, b] - first, b, b + 2 * WB)]
            chosen = jnp.where(k < counts[b], chosen, jnp.zeros((), bf16))
            total += lax.dot_general(dip_v[b, k], chosen, NT, preferred_element_type=f32)
        total = jnp.where(kept < lens[b], total, 0.0)
        stage[pl.ds(b, sub, stride=PAD), :] = total
    msg[...] = stage[...].astype(bf16).reshape(msg.shape)

    def send_piece(i, carry):
        to = lax.rem(row + i, n_row)
        pltpu.make_async_remote_copy(
            src_ref=msg.at[to], dst_ref=recv.at[row],
            send_sem=a2a_send, recv_sem=a2a_recv,
            device_id=(to, col), device_id_type=MESH,
        ).start()
        return carry

    lax.fori_loop(1, n_row, send_piece, 0)
    recv[row] = msg[row]
    many = pl.ds(0, n_row - 1)
    pltpu.make_async_copy(recv.at[many], recv.at[many], a2a_recv).wait()

    rows = recv[...].reshape(n_row * PAD, st)
    turned = lax.dot_general(
        rows, select, (((0,), (0,)), ((), ())), preferred_element_type=f32
    ).astype(bf16)
    half = st // 2
    gath[col, 0:st, :] = turned[:, 0:128]
    gath[col, st : 2 * st, :] = turned[:, 128:256]
    gath[col, 2 * st : 2 * st + half, :] = jnp.concatenate(
        [turned[:half, 256:320], turned[half:, 256:320]], axis=1
    )

    hops = [(s + 1) // 2 if s % 2 else n_col - s // 2 for s in range(1, n_col)]
    for d in hops:
        pltpu.make_async_remote_copy(
            src_ref=gath.at[col], dst_ref=gath.at[col],
            send_sem=z_send, recv_sem=z_recv.at[col],
            device_id=(row, lax.rem(col + d, n_col)), device_id_type=MESH,
        ).start()
    ld_eig.wait()

    cols = eig_v.shape[1]
    width = 256
    shards = cols // width
    for step, d in enumerate([0] + hops):
        c = lax.rem(col + n_col - d, n_col)
        if d:
            pltpu.make_async_copy(gath.at[c], gath.at[c], z_recv.at[c]).wait()
        base = pl.multiple_of(c * piece, 64)
        lhs_a = jnp.concatenate([gath[c, 0:st, :], gath[c, st : 2 * st, :]], axis=1)
        tail = gath[c, 2 * st : 2 * st + half, :]
        lhs_b = jnp.concatenate([tail[:, 0:64], tail[:, 64:128]], axis=0)
        for n in range(shards):
            span = slice(n * width, (n + 1) * width)
            part = jnp.dot(lhs_a, eig_v[pl.ds(base, 256), span], preferred_element_type=f32)
            part += jnp.dot(lhs_b, eig_v[pl.ds(base + 256, 64), span], preferred_element_type=f32)
            if step:
                part += acc[:, span]
            acc[:, span] = part
            if step == n_col - 1:

                def send_shard(i, carry, n=n):
                    group = lax.rem(row // shards + i, n_row // shards)
                    to = group * shards + n

                    @pl.when(to != row)
                    def _():
                        pltpu.make_async_remote_copy(
                            src_ref=acc.at[pl.ds(pl.multiple_of(group * 8, 8), 8), pl.ds(n * width, width)],
                            dst_ref=rs_recv.at[row],
                            send_sem=rs_send, recv_sem=rs_sem,
                            device_id=(to, col), device_id_type=MESH,
                        ).start()

                    return carry

                lax.fori_loop(0, n_row // shards, send_shard, 0)

    mine = (
        pl.ds(pl.multiple_of((row // shards) * 8, 8), 8),
        pl.ds(pl.multiple_of(lax.rem(row, shards) * width, width), width),
    )
    rs_recv[row] = acc[mine]
    pltpu.make_async_copy(rs_recv.at[many], rs_recv.at[many], rs_sem).wait()
    out_ref[mine] = jnp.sum(rs_recv[...], axis=0)

    def send_result(i, carry):
        pltpu.make_async_remote_copy(
            src_ref=out_ref.at[mine], dst_ref=out_ref.at[mine],
            send_sem=ag_send, recv_sem=ag_sem,
            device_id=(lax.rem(row + i, n_row), col), device_id_type=MESH,
        ).start()
        return carry

    lax.fori_loop(1, n_row, send_result, 0)
    others = gath.at[pl.ds(0, n_col - 1)]
    pltpu.make_async_copy(recv.at[many], recv.at[many], a2a_send).wait()
    pltpu.make_async_copy(others, others, z_send).wait()
    pltpu.make_async_copy(rs_recv.at[many], rs_recv.at[many], rs_send).wait()
    pltpu.make_async_copy(rs_recv.at[many], rs_recv.at[many], ag_sem).wait()
    pltpu.make_async_copy(rs_recv.at[many], rs_recv.at[many], ag_send).wait()


def on_device(n_row, n_col, psi, block_len, targets, counts, dipole, eigvec):
    nb, kmax, _, bs = dipole.shape
    st = psi.shape[1]
    rows, cols = eigvec.shape
    piece = nb * n_row
    bf16, f32 = jnp.bfloat16, jnp.float32
    dma = pltpu.SemaphoreType.DMA
    smem = pl.BlockSpec(memory_space=pltpu.SMEM)
    hbm = pl.BlockSpec(memory_space=pl.ANY)
    turned = pl.pallas_call(
        functools.partial(body, n_row, n_col, nb, kmax, bs, st),
        out_shape=jax.ShapeDtypeStruct((st, cols), f32),
        in_specs=[smem] * 3 + [hbm] * 3,
        out_specs=pl.BlockSpec(memory_space=pltpu.VMEM),
        scratch_shapes=[
            pltpu.VMEM((st, nb * bs), bf16),
            pltpu.VMEM((nb + 2 * WB, st, bs), bf16),
            pltpu.VMEM(dipole.shape, bf16),
            pltpu.VMEM((rows, cols), bf16),
            pltpu.VMEM((n_row * PAD, st), f32),
            pltpu.VMEM((n_row, PAD, st), bf16),
            pltpu.VMEM((n_row, PAD, st), bf16),
            pltpu.VMEM((n_col, piece // 2, 128), bf16),
            pltpu.VMEM((st, cols), f32),
            pltpu.VMEM((n_row, 8, 256), f32),
            dma((3,)),
            dma((2,)),
            dma((2,)),
            dma,
            dma,
            dma,
            dma((n_col,)),
            dma,
            dma,
            dma,
            dma,
        ],
        compiler_params=pltpu.CompilerParams(
            collective_id=0, has_side_effects=True, vmem_limit_bytes=56 * 2**20
        ),
    )(block_len, targets.T, counts, psi.T, dipole, eigvec)
    return turned.T


def solution(mesh):
    placed = (
        P("row", None),
        P("row"),
        P("row", None),
        P("row"),
        P("row", None, "col", None),
        P("row", "col"),
    )
    return jax.shard_map(
        functools.partial(on_device, mesh.shape["row"], mesh.shape["col"]),
        mesh=mesh, in_specs=placed, out_specs=P("col", None), check_vma=False,
    )
```

```python
import functools

import jax
import jax.numpy as jnp
from jax import lax
from jax.experimental import pallas as pl
from jax.experimental.pallas import tpu as pltpu
from jax.sharding import PartitionSpec as P

WB = 2
MESH = pl.DeviceIdType.MESH
NT = (((1,), (1,)), ((), ()))
TN = (((0,), (0,)), ((), ()))
PAD = 16
HALVES = 2


def body(
    n_row, n_col, nb, kmax, bs, st,
    lens_hbm, targets_hbm, counts_hbm, psi_hbm, dip_hbm, eig_hbm, out_ref,
    lens, targets, counts, psi_v, own, low, high, dip_v, eig_v, eig_p,
    stage, msg, recv, inner, edge, acc, rs_recv,
    ld_sem, halo_send, halo_recv, a2a_send, a2a_recv, z_send, z_recv, ze_send, ze_recv,
    rs_send, rs_sem, ag_send, ag_sem,
):
    row = lax.axis_index("row")
    col = lax.axis_index("col")
    f32, bf16 = jnp.float32, jnp.bfloat16
    n_edge = 2 * WB
    n_inner = nb - n_edge
    piece = nb * n_row
    k_edge = n_edge * n_row
    k_inner = n_inner * n_row
    cols = eig_v.shape[1]
    half = st // HALVES

    loads = [
        pltpu.make_async_copy(src, dst, ld_sem.at[i])
        for i, (src, dst) in enumerate(
            [
                (lens_hbm, lens),
                (targets_hbm, targets),
                (counts_hbm, counts),
                (psi_hbm, psi_v),
                (dip_hbm, dip_v),
                (eig_hbm, eig_v),
            ]
        )
    ]
    for load in loads:
        load.start()

    barrier = pltpu.get_barrier_semaphore()

    def greet_row(i, carry):
        pl.semaphore_signal(
            barrier, inc=1, device_id=(lax.rem(row + i, n_row), col), device_id_type=MESH
        )
        return carry

    def greet_col(i, carry):
        pl.semaphore_signal(
            barrier, inc=1, device_id=(row, lax.rem(col + i, n_col)), device_id_type=MESH
        )
        return carry

    lax.fori_loop(1, n_row, greet_row, 0)
    lax.fori_loop(1, n_col, greet_col, 0)

    stage[...] = jnp.zeros_like(stage)
    for load in loads[:4]:
        load.wait()

    lane = lax.broadcasted_iota(jnp.int32, (st, bs), 1)
    for b in range(nb):
        block = jnp.where(
            lane < lens[b], psi_v[:, b * bs : (b + 1) * bs], jnp.zeros((), bf16)
        )
        own[b] = block
        if b < 2 * WB:
            low[WB + b] = block
        if b >= nb - 2 * WB:
            high[b - (nb - 2 * WB)] = block
    loads[4].wait()

    kept = lax.broadcasted_iota(jnp.int32, (n_row, st), 0) + col * n_row

    def product(b, blocks, base, at, part):
        top = blocks.shape[0] - 1
        total = jnp.zeros((n_row, st), f32)
        for k in range(kmax):
            chosen = blocks[jnp.clip(targets[k, b] - (row * nb + base), 0, top)]
            chosen = jnp.where(k < counts[b], chosen, jnp.zeros((), bf16))
            total += lax.dot_general(dip_v[b, k], chosen, NT, preferred_element_type=f32)
        total = jnp.where(kept < lens[b], total, 0.0)
        stage[part, pl.ds(at, n_row, stride=PAD), :] = total

    def send_pieces(part):
        msg[part] = stage[part].astype(bf16).reshape(n_row, PAD, st)

        def send(i, carry):
            to = lax.rem(row + i, n_row)
            pltpu.make_async_remote_copy(
                src_ref=msg.at[part, to], dst_ref=recv.at[part, row],
                send_sem=a2a_send.at[part], recv_sem=a2a_recv.at[part],
                device_id=(to, col), device_id_type=MESH,
            ).start()
            return carry

        lax.fori_loop(1, n_row, send, 0)
        recv[part, row] = msg[part, row]

    many = pl.ds(0, n_row - 1)

    def collect(part, count):
        pltpu.make_async_copy(
            recv.at[part, many], recv.at[part, many], a2a_recv.at[part]
        ).wait()
        shape = (n_row * PAD, count * n_row)
        wanted = lax.broadcasted_iota(jnp.int32, shape, 1)
        wanted = wanted + (PAD - count) * (wanted // count)
        select = jnp.where(lax.broadcasted_iota(jnp.int32, shape, 0) == wanted, 1.0, 0.0)
        rows = recv[part].reshape(n_row * PAD, st)
        return lax.dot_general(
            rows, select.astype(bf16), TN, preferred_element_type=f32
        ).astype(bf16)

    for at in range(n_inner):
        product(WB + at, own, 0, at, 0)

    pl.semaphore_wait(barrier, n_row - 1 + n_col - 1)

    to_right = pltpu.make_async_remote_copy(
        src_ref=own.at[pl.ds(nb - WB, WB)], dst_ref=low.at[pl.ds(0, WB)],
        send_sem=halo_send.at[0], recv_sem=halo_recv.at[0],
        device_id=(lax.rem(row + 1, n_row), col), device_id_type=MESH,
    )
    to_left = pltpu.make_async_remote_copy(
        src_ref=own.at[pl.ds(0, WB)], dst_ref=high.at[pl.ds(2 * WB, WB)],
        send_sem=halo_send.at[1], recv_sem=halo_recv.at[1],
        device_id=(lax.rem(row + n_row - 1, n_row), col), device_id_type=MESH,
    )
    to_right.start()
    to_left.start()
    send_pieces(0)

    loads[5].wait()
    place = lax.broadcasted_iota(jnp.int32, (piece, piece), 0)
    group, at = place // n_edge, place % n_edge
    from_edge = group * nb + at + jnp.where(at >= WB, n_inner, 0)
    inner_place = place - k_edge
    from_inner = (inner_place // n_inner) * nb + WB + inner_place % n_inner
    source = jnp.where(place < k_edge, from_edge, from_inner)
    permute = jnp.where(
        lax.broadcasted_iota(jnp.int32, (piece, piece), 1) == source, 1.0, 0.0
    ).astype(bf16)
    for c in range(n_col):
        span = slice(c * piece, (c + 1) * piece)
        eig_p[span, :] = jnp.dot(
            permute, eig_v[span, :], preferred_element_type=f32
        ).astype(bf16)

    to_right.wait()
    to_left.wait()
    for at in range(WB):
        product(at, low, -WB, at, 1)
    for at in range(WB):
        product(nb - WB + at, high, nb - 2 * WB, WB + at, 1)
    send_pieces(1)

    hops = [(s + 1) // 2 if s % 2 else n_col - s // 2 for s in range(1, n_col)]
    turned = collect(0, n_inner)
    inner[col, 0:st, :] = turned[:, 0:128]
    inner[col, st : st + st // 2, :] = jnp.concatenate(
        [turned[: st // 2, 128:k_inner], turned[st // 2 :, 128:k_inner]], axis=1
    )
    for d in hops:
        pltpu.make_async_remote_copy(
            src_ref=inner.at[col], dst_ref=inner.at[col],
            send_sem=z_send, recv_sem=z_recv.at[col],
            device_id=(row, lax.rem(col + d, n_col)), device_id_type=MESH,
        ).start()

    turned = collect(1, n_edge)
    for h in range(HALVES):
        edge[h, col] = turned[h * half : (h + 1) * half, :]
        for d in hops:
            pltpu.make_async_remote_copy(
                src_ref=edge.at[h, col], dst_ref=edge.at[h, col],
                send_sem=ze_send.at[h], recv_sem=ze_recv.at[h, col],
                device_id=(row, lax.rem(col + d, n_col)), device_id_type=MESH,
            ).start()

    for d in [0] + hops:
        c = lax.rem(col + n_col - d, n_col)
        if d:
            pltpu.make_async_copy(inner.at[c], inner.at[c], z_recv.at[c]).wait()
        tail = inner[c, st : st + st // 2, :]
        tail = jnp.concatenate([tail[:, 0:64], tail[:, 64:128]], axis=0)
        lhs = jnp.concatenate([inner[c, 0:st, :], tail], axis=1)
        base = pl.multiple_of(c * piece + k_edge, 64)
        part = jnp.dot(lhs, eig_p[pl.ds(base, k_inner), :], preferred_element_type=f32)
        acc[...] = acc[...] + part if d else part

    lanes = cols // 128
    tile = (
        pl.ds(pl.multiple_of((row // lanes) * 8, 8), 8),
        pl.ds(pl.multiple_of(lax.rem(row, lanes) * 128, 128), 128),
    )
    for h in range(HALVES):
        low_row = h * half
        for d in [0] + hops:
            c = lax.rem(col + n_col - d, n_col)
            if d:
                pltpu.make_async_copy(edge.at[h, c], edge.at[h, c], ze_recv.at[h, c]).wait()
            base = pl.multiple_of(c * piece, 64)
            acc[low_row : low_row + half, :] += jnp.dot(
                edge[h, c], eig_p[pl.ds(base, k_edge), :], preferred_element_type=f32
            )

        def send_tile(i, carry, h=h, low_row=low_row):
            to = lax.rem(row + i, n_row)
            at_row = pl.multiple_of(low_row + (to // lanes) * 8, 8)
            at_lane = pl.multiple_of(lax.rem(to, lanes) * 128, 128)
            pltpu.make_async_remote_copy(
                src_ref=acc.at[pl.ds(at_row, 8), pl.ds(at_lane, 128)],
                dst_ref=rs_recv.at[h, row],
                send_sem=rs_send.at[h], recv_sem=rs_sem.at[h],
                device_id=(to, col), device_id_type=MESH,
            ).start()
            return carry

        lax.fori_loop(1, n_row, send_tile, 0)
        rs_recv[h, row] = acc[
            pl.ds(pl.multiple_of(low_row + (row // lanes) * 8, 8), 8), tile[1]
        ]

    for h in range(HALVES):
        pltpu.make_async_copy(
            rs_recv.at[h, many], rs_recv.at[h, many], rs_sem.at[h]
        ).wait()
        mine = (pl.ds(pl.multiple_of(h * half + (row // lanes) * 8, 8), 8), tile[1])
        out_ref[mine] = jnp.sum(rs_recv[h], axis=0)

        def send_result(i, carry, h=h, mine=mine):
            pltpu.make_async_remote_copy(
                src_ref=out_ref.at[mine], dst_ref=out_ref.at[mine],
                send_sem=ag_send.at[h], recv_sem=ag_sem.at[h],
                device_id=(lax.rem(row + i, n_row), col), device_id_type=MESH,
            ).start()
            return carry

        lax.fori_loop(1, n_row, send_result, 0)

    others = pl.ds(0, n_col - 1)
    pltpu.make_async_copy(inner.at[others], inner.at[others], z_send).wait()
    for h in range(HALVES):
        pltpu.make_async_copy(recv.at[h, many], recv.at[h, many], a2a_send.at[h]).wait()
        pltpu.make_async_copy(edge.at[h, others], edge.at[h, others], ze_send.at[h]).wait()
        pltpu.make_async_copy(rs_recv.at[h, many], rs_recv.at[h, many], rs_send.at[h]).wait()
    for h in range(HALVES):
        pltpu.make_async_copy(rs_recv.at[h, many], rs_recv.at[h, many], ag_sem.at[h]).wait()
        pltpu.make_async_copy(rs_recv.at[h, many], rs_recv.at[h, many], ag_send.at[h]).wait()


def on_device(n_row, n_col, psi, block_len, targets, counts, dipole, eigvec):
    nb, kmax, _, bs = dipole.shape
    st = psi.shape[1]
    rows, cols = eigvec.shape
    n_edge, n_inner = 2 * WB, nb - 2 * WB
    bf16, f32, i32 = jnp.bfloat16, jnp.float32, jnp.int32
    dma = pltpu.SemaphoreType.DMA
    operands = [
        pltpu.with_memory_space_constraint(a, pltpu.HBM)
        for a in (block_len, targets.T, counts, psi.T, dipole, eigvec)
    ]
    turned = pl.pallas_call(
        functools.partial(body, n_row, n_col, nb, kmax, bs, st),
        out_shape=jax.ShapeDtypeStruct((st, cols), f32),
        in_specs=[pl.BlockSpec(memory_space=pltpu.HBM)] * 6,
        out_specs=pl.BlockSpec(memory_space=pltpu.VMEM),
        scratch_shapes=[
            pltpu.SMEM((nb,), i32),
            pltpu.SMEM((kmax, nb), i32),
            pltpu.SMEM((nb,), i32),
            pltpu.VMEM((st, nb * bs), bf16),
            pltpu.VMEM((nb, st, bs), bf16),
            pltpu.VMEM((3 * WB, st, bs), bf16),
            pltpu.VMEM((3 * WB, st, bs), bf16),
            pltpu.VMEM(dipole.shape, bf16),
            pltpu.VMEM((rows, cols), bf16),
            pltpu.VMEM((rows, cols), bf16),
            pltpu.VMEM((2, n_row * PAD, st), f32),
            pltpu.VMEM((2, n_row, PAD, st), bf16),
            pltpu.VMEM((2, n_row, PAD, st), bf16),
            pltpu.VMEM((n_col, n_inner * n_row // 2, 128), bf16),
            pltpu.VMEM((HALVES, n_col, st // HALVES, n_edge * n_row), bf16),
            pltpu.VMEM((st, cols), f32),
            pltpu.VMEM((HALVES, n_row, 8, 128), f32),
            dma((6,)),
            dma((2,)),
            dma((2,)),
            dma((2,)),
            dma((2,)),
            dma,
            dma((n_col,)),
            dma((HALVES,)),
            dma((HALVES, n_col)),
            dma((HALVES,)),
            dma((HALVES,)),
            dma((HALVES,)),
            dma((HALVES,)),
        ],
        compiler_params=pltpu.CompilerParams(
            collective_id=0, has_side_effects=True, vmem_limit_bytes=24 * 2**20
        ),
    )(*operands)
    return turned.T


def solution(mesh):
    placed = (
        P("row", None),
        P("row"),
        P("row", None),
        P("row"),
        P("row", None, "col", None),
        P("row", "col"),
    )
    return jax.shard_map(
        functools.partial(on_device, mesh.shape["row"], mesh.shape["col"]),
        mesh=mesh, in_specs=placed, out_specs=P("col", None), check_vma=False,
    )
```

```python
import functools

import jax
import jax.numpy as jnp
from jax import lax
from jax.experimental import pallas as pl
from jax.experimental.pallas import tpu as pltpu
from jax.sharding import PartitionSpec as P

WB = 2
MESH = pl.DeviceIdType.MESH
NT = (((1,), (1,)), ((), ()))
TN = (((0,), (0,)), ((), ()))
HALVES = 2


def body(
    n_row, n_col, nb, kmax, bs, st,
    lens_hbm, targets_hbm, counts_hbm, psi_hbm, dip_hbm, eig_hbm, out_ref,
    lens, targets, counts, psi_v, own, low, high, dip_v, eig_v, eig_p,
    inner_msg, edge_msg, inner_recv, edge_recv, inner, edge, acc, rs_recv,
    ld_sem, halo_send, halo_recv, a2a_send, a2a_recv, z_send, z_recv, ze_send, ze_recv,
    rs_send, rs_sem, ag_send, ag_sem,
):
    row = lax.axis_index("row")
    col = lax.axis_index("col")
    f32, bf16 = jnp.float32, jnp.bfloat16
    n_edge = 2 * WB
    n_inner = nb - n_edge
    piece = nb * n_row
    k_edge = n_edge * n_row
    k_inner = n_inner * n_row
    cols = eig_v.shape[1]
    half = st // HALVES

    loads = [
        pltpu.make_async_copy(src, dst, ld_sem.at[i])
        for i, (src, dst) in enumerate(
            [
                (lens_hbm, lens),
                (targets_hbm, targets),
                (counts_hbm, counts),
                (psi_hbm, psi_v),
                (dip_hbm, dip_v),
                (eig_hbm, eig_v),
            ]
        )
    ]

    chip_x, chip_y, core = row // 8, lax.rem(row // 2, 4), lax.rem(row, 2)
    at_x = [lax.rem(chip_x + d, 4) for d in range(4)]
    at_y = [[lax.rem(chip_y + d, 4) * 2 + c for c in (core, 1 - core)] for d in range(4)]
    offsets = [(x, y, c) for x in range(4) for y in range(4) for c in range(2)][1:]
    offsets.sort(key=lambda o: -(min(o[0], 4 - o[0]) + min(o[1], 4 - o[1])))
    peers = [(at_x[x], at_y[y][c]) for x, y, c in offsets]

    barrier = pltpu.get_barrier_semaphore()

    for x, y in peers:
        pl.semaphore_signal(
            barrier, inc=1, device_id=(x * 8 + y, col), device_id_type=MESH
        )
    for i in range(1, n_col):
        pl.semaphore_signal(
            barrier, inc=1, device_id=(row, lax.rem(col + i, n_col)), device_id_type=MESH
        )
    for load in loads:
        load.start()

    def rows_are(count, wanted):
        held = lax.broadcasted_iota(jnp.int32, (count, wanted.shape[1]), 0)
        return jnp.where(held == wanted, 1.0, 0.0).astype(bf16)

    def kept_rows(used, held):
        at = lax.broadcasted_iota(jnp.int32, (1, used * n_row), 1)
        return rows_are(held * n_row, at + (held - used) * (at // used))

    select_inner = kept_rows(n_inner // 2, inner_msg.shape[1])
    select_edge = kept_rows(WB, edge_msg.shape[1])
    at = lax.broadcasted_iota(jnp.int32, (1, piece), 1)
    group, at = at // nb, at % nb
    late = at >= nb - WB
    at_edge = jnp.where(late, at - (nb - WB), at)
    to_edge = at_edge * (k_edge // 2) + group * 2 + jnp.where(late, 1, 0)
    at_inner = at - WB
    third = n_inner // 2
    to_inner = (at_inner // third) * (k_inner // 2) + group * third + at_inner % third
    permute = rows_are(piece, jnp.where((at < WB) | late, to_edge, k_edge + to_inner))

    for r in range(third, inner_msg.shape[1]):
        inner_msg[:, r, :] = jnp.zeros((n_row, 128), f32)
    for load in loads[:4]:
        load.wait()

    lane = lax.broadcasted_iota(jnp.int32, (st, bs), 1)
    for b in range(nb):
        block = jnp.where(
            lane < lens[b], psi_v[:, b * bs : (b + 1) * bs], jnp.zeros((), bf16)
        )
        own[b] = block
        if b < 2 * WB:
            low[WB + b] = block
        if b >= nb - 2 * WB:
            high[b - (nb - 2 * WB)] = block
    loads[4].wait()

    kept = lax.broadcasted_iota(jnp.int32, (n_row, st), 0) + col * n_row

    def product(b, blocks, base):
        top = blocks.shape[0] - 1
        total = jnp.zeros((n_row, st), f32)
        for k in range(kmax):
            chosen = blocks[jnp.clip(targets[k, b] - (row * nb + base), 0, top)]
            chosen = jnp.where(k < counts[b], chosen, jnp.zeros((), bf16))
            total += lax.dot_general(dip_v[b, k], chosen, NT, preferred_element_type=f32)
        return jnp.where(kept < lens[b], total, 0.0).astype(bf16).astype(f32)

    def send_pieces(part, msg, recv):
        for x, y in peers:
            to = x * 8 + y
            pltpu.make_async_remote_copy(
                src_ref=msg.at[to], dst_ref=recv.at[row],
                send_sem=a2a_send.at[part], recv_sem=a2a_recv.at[part],
                device_id=(to, col), device_id_type=MESH,
            ).start()
        recv[row] = msg[row]

    many = pl.ds(0, n_row - 1)

    def collect(part, recv, select):
        pltpu.make_async_copy(recv.at[many], recv.at[many], a2a_recv.at[part]).wait()
        rows = recv[...].reshape(-1, 128).astype(bf16)
        both = lax.dot_general(rows, select, TN, preferred_element_type=f32).astype(bf16)
        return jnp.concatenate([both[:st], both[st:]], axis=1)

    for r in range(third):
        inner_msg[:, r, :] = jnp.concatenate(
            [product(WB + r, own, 0), product(WB + third + r, own, 0)], axis=1
        )

    pl.semaphore_wait(barrier, n_row - 1 + n_col - 1)

    to_right = pltpu.make_async_remote_copy(
        src_ref=own.at[pl.ds(nb - WB, WB)], dst_ref=low.at[pl.ds(0, WB)],
        send_sem=halo_send.at[0], recv_sem=halo_recv.at[0],
        device_id=(lax.rem(row + 1, n_row), col), device_id_type=MESH,
    )
    to_left = pltpu.make_async_remote_copy(
        src_ref=own.at[pl.ds(0, WB)], dst_ref=high.at[pl.ds(2 * WB, WB)],
        send_sem=halo_send.at[1], recv_sem=halo_recv.at[1],
        device_id=(lax.rem(row + n_row - 1, n_row), col), device_id_type=MESH,
    )
    to_right.start()
    to_left.start()
    send_pieces(0, inner_msg, inner_recv)

    loads[5].wait()
    for c in range(n_col):
        span = slice(c * piece, (c + 1) * piece)
        eig_p[span, :] = jnp.dot(
            permute, eig_v[span, :], preferred_element_type=f32
        ).astype(bf16)

    to_right.wait()
    to_left.wait()
    edge_msg[:, 0, :] = jnp.concatenate([product(b, low, -WB) for b in range(WB)], axis=1)
    edge_msg[:, 1, :] = jnp.concatenate(
        [product(b, high, nb - 2 * WB) for b in range(nb - WB, nb)], axis=1
    )
    send_pieces(1, edge_msg, edge_recv)

    hops = [(s + 1) // 2 if s % 2 else n_col - s // 2 for s in range(1, n_col)]
    far_first = hops[::-1]
    turned = collect(0, inner_recv, select_inner)
    inner[col, 0:st, :] = turned[:, 0:128]
    inner[col, st : st + st // 2, :] = jnp.concatenate(
        [turned[: st // 2, 128:k_inner], turned[st // 2 :, 128:k_inner]], axis=1
    )
    for d in far_first:
        pltpu.make_async_remote_copy(
            src_ref=inner.at[col], dst_ref=inner.at[col],
            send_sem=z_send, recv_sem=z_recv.at[col],
            device_id=(row, lax.rem(col + d, n_col)), device_id_type=MESH,
        ).start()

    turned = collect(1, edge_recv, select_edge)
    for h in range(HALVES):
        edge[h, col] = turned[h * half : (h + 1) * half, :]
        for d in far_first:
            pltpu.make_async_remote_copy(
                src_ref=edge.at[h, col], dst_ref=edge.at[h, col],
                send_sem=ze_send.at[h], recv_sem=ze_recv.at[h, col],
                device_id=(row, lax.rem(col + d, n_col)), device_id_type=MESH,
            ).start()

    for d in [0] + hops:
        c = lax.rem(col + n_col - d, n_col)
        if d:
            pltpu.make_async_copy(inner.at[c], inner.at[c], z_recv.at[c]).wait()
        tail = inner[c, st : st + st // 2, :]
        tail = jnp.concatenate([tail[:, 0:64], tail[:, 64:128]], axis=0)
        lhs = jnp.concatenate([inner[c, 0:st, :], tail], axis=1)
        base = pl.multiple_of(c * piece + k_edge, 64)
        part = jnp.dot(lhs, eig_p[pl.ds(base, k_inner), :], preferred_element_type=f32)
        acc[...] = acc[...] + part if d else part

    lanes = cols // 128
    tile = (
        pl.ds(pl.multiple_of((row // lanes) * 8, 8), 8),
        pl.ds(pl.multiple_of(lax.rem(row, lanes) * 128, 128), 128),
    )
    for h in range(HALVES):
        low_row = h * half
        for d in [0] + hops:
            c = lax.rem(col + n_col - d, n_col)
            if d:
                pltpu.make_async_copy(edge.at[h, c], edge.at[h, c], ze_recv.at[h, c]).wait()
            base = pl.multiple_of(c * piece, 64)
            acc[low_row : low_row + half, :] += jnp.dot(
                edge[h, c], eig_p[pl.ds(base, k_edge), :], preferred_element_type=f32
            )

        for x, y in peers:
            at_row = pl.multiple_of(low_row + x * 8, 8)
            at_lane = pl.multiple_of(y * 128, 128)
            pltpu.make_async_remote_copy(
                src_ref=acc.at[pl.ds(at_row, 8), pl.ds(at_lane, 128)],
                dst_ref=rs_recv.at[h, row],
                send_sem=rs_send.at[h], recv_sem=rs_sem.at[h],
                device_id=(x * 8 + y, col), device_id_type=MESH,
            ).start()
        rs_recv[h, row] = acc[
            pl.ds(pl.multiple_of(low_row + (row // lanes) * 8, 8), 8), tile[1]
        ]

    for h in range(HALVES):
        pltpu.make_async_copy(
            rs_recv.at[h, many], rs_recv.at[h, many], rs_sem.at[h]
        ).wait()
        mine = (pl.ds(pl.multiple_of(h * half + (row // lanes) * 8, 8), 8), tile[1])
        out_ref[mine] = jnp.sum(rs_recv[h], axis=0)

        for x, y in peers:
            pltpu.make_async_remote_copy(
                src_ref=out_ref.at[mine], dst_ref=out_ref.at[mine],
                send_sem=ag_send.at[h], recv_sem=ag_sem.at[h],
                device_id=(x * 8 + y, col), device_id_type=MESH,
            ).start()

    others = pl.ds(0, n_col - 1)
    pltpu.make_async_copy(inner.at[others], inner.at[others], z_send).wait()
    for h in range(HALVES):
        sent = (inner_msg, edge_msg)[h].at[many]
        pltpu.make_async_copy(sent, sent, a2a_send.at[h]).wait()
        pltpu.make_async_copy(edge.at[h, others], edge.at[h, others], ze_send.at[h]).wait()
        pltpu.make_async_copy(rs_recv.at[h, many], rs_recv.at[h, many], rs_send.at[h]).wait()
    for h in range(HALVES):
        pltpu.make_async_copy(rs_recv.at[h, many], rs_recv.at[h, many], ag_sem.at[h]).wait()
        pltpu.make_async_copy(rs_recv.at[h, many], rs_recv.at[h, many], ag_send.at[h]).wait()


def on_device(n_row, n_col, psi, block_len, targets, counts, dipole, eigvec):
    nb, kmax, _, bs = dipole.shape
    st = psi.shape[1]
    rows, cols = eigvec.shape
    n_edge, n_inner = 2 * WB, nb - 2 * WB
    bf16, f32, i32 = jnp.bfloat16, jnp.float32, jnp.int32
    dma = pltpu.SemaphoreType.DMA
    operands = [
        pltpu.with_memory_space_constraint(a, pltpu.HBM)
        for a in (block_len, targets.T, counts, psi.T, dipole, eigvec)
    ]
    turned = pl.pallas_call(
        functools.partial(body, n_row, n_col, nb, kmax, bs, st),
        out_shape=jax.ShapeDtypeStruct((st, cols), f32),
        in_specs=[pl.BlockSpec(memory_space=pltpu.HBM)] * 6,
        out_specs=pl.BlockSpec(memory_space=pltpu.VMEM),
        scratch_shapes=[
            pltpu.SMEM((nb,), i32),
            pltpu.SMEM((kmax, nb), i32),
            pltpu.SMEM((nb,), i32),
            pltpu.VMEM((st, nb * bs), bf16),
            pltpu.VMEM((nb, st, bs), bf16),
            pltpu.VMEM((3 * WB, st, bs), bf16),
            pltpu.VMEM((3 * WB, st, bs), bf16),
            pltpu.VMEM(dipole.shape, bf16),
            pltpu.VMEM((rows, cols), bf16),
            pltpu.VMEM((rows, cols), bf16),
            pltpu.VMEM((n_row, 4, 128), f32),
            pltpu.VMEM((n_row, 2, 128), f32),
            pltpu.VMEM((n_row, 4, 128), f32),
            pltpu.VMEM((n_row, 2, 128), f32),
            pltpu.VMEM((n_col, n_inner * n_row // 2, 128), bf16),
            pltpu.VMEM((HALVES, n_col, st // HALVES, n_edge * n_row), bf16),
            pltpu.VMEM((st, cols), f32),
            pltpu.VMEM((HALVES, n_row, 8, 128), f32),
            dma((6,)),
            dma((2,)),
            dma((2,)),
            dma((2,)),
            dma((2,)),
            dma,
            dma((n_col,)),
            dma((HALVES,)),
            dma((HALVES, n_col)),
            dma((HALVES,)),
            dma((HALVES,)),
            dma((HALVES,)),
            dma((HALVES,)),
        ],
        compiler_params=pltpu.CompilerParams(
            collective_id=0, has_side_effects=True, vmem_limit_bytes=24 * 2**20
        ),
    )(*operands)
    return turned.T


def solution(mesh):
    placed = (
        P("row", None),
        P("row"),
        P("row", None),
        P("row"),
        P("row", None, "col", None),
        P("row", "col"),
    )
    return jax.shard_map(
        functools.partial(on_device, mesh.shape["row"], mesh.shape["col"]),
        mesh=mesh, in_specs=placed, out_specs=P("col", None), check_vma=False,
    )
```

```python
import functools

import jax
import jax.numpy as jnp
from jax import lax
from jax.experimental import pallas as pl
from jax.experimental.pallas import tpu as pltpu
from jax.sharding import PartitionSpec as P

WB = 2
MESH = pl.DeviceIdType.MESH
NT = (((1,), (1,)), ((), ()))
TN = (((0,), (0,)), ((), ()))
HALVES = 2


def body(
    n_row, n_col, nb, kmax, bs, st,
    lens_hbm, targets_hbm, counts_hbm, psi_hbm, dip_hbm, eig_hbm, out_ref,
    lens, targets, counts, psi_v, own, low, high, dip_v, eig_v, eig_p,
    inner_msg, edge_msg, inner_recv, edge_recv, inner, edge, acc, rs_recv,
    ld_sem, halo_send, halo_recv, a2a_send, a2a_recv, z_send, z_recv, ze_send, ze_recv,
    rs_send, rs_sem, ag_send, ag_sem,
):
    row = lax.axis_index("row")
    col = lax.axis_index("col")
    f32, bf16 = jnp.float32, jnp.bfloat16
    n_edge = 2 * WB
    n_inner = nb - n_edge
    piece = nb * n_row
    k_edge = n_edge * n_row
    k_inner = n_inner * n_row
    cols = eig_v.shape[1]
    half = st // HALVES

    loads = [
        pltpu.make_async_copy(src, dst, ld_sem.at[i])
        for i, (src, dst) in enumerate(
            [
                (lens_hbm, lens),
                (targets_hbm, targets),
                (counts_hbm, counts),
                (psi_hbm, psi_v),
                (dip_hbm, dip_v),
                (eig_hbm, eig_v),
            ]
        )
    ]

    chip_x, chip_y, core = row // 8, lax.rem(row // 2, 4), lax.rem(row, 2)
    at_x = [lax.rem(chip_x + d, 4) for d in range(4)]
    at_y = [[lax.rem(chip_y + d, 4) * 2 + c for c in (core, 1 - core)] for d in range(4)]
    offsets = [(x, y, c) for x in range(4) for y in range(4) for c in range(2)][1:]
    offsets.sort(key=lambda o: -(min(o[0], 4 - o[0]) + min(o[1], 4 - o[1])))
    peers = [(at_x[x], at_y[y][c]) for x, y, c in offsets]

    barrier = pltpu.get_barrier_semaphore()

    for x, y in peers:
        pl.semaphore_signal(
            barrier, inc=1, device_id=(x * 8 + y, col), device_id_type=MESH
        )
    for i in range(1, n_col):
        pl.semaphore_signal(
            barrier, inc=1, device_id=(row, lax.rem(col + i, n_col)), device_id_type=MESH
        )
    for load in loads:
        load.start()

    def rows_are(count, wanted):
        held = lax.broadcasted_iota(jnp.int32, (count, wanted.shape[1]), 0)
        return jnp.where(held == wanted, 1.0, 0.0).astype(bf16)

    def kept_rows(used, held):
        at = lax.broadcasted_iota(jnp.int32, (1, used * n_row), 1)
        return rows_are(held * n_row, at + (held - used) * (at // used))

    select_inner = kept_rows(n_inner // 2, inner_msg.shape[1])
    at = lax.broadcasted_iota(jnp.int32, (1, piece), 1)
    group, at = at // nb, at % nb
    late = at >= nb - WB
    at_edge = jnp.where(late, at - (nb - WB), at)
    to_edge = at_edge * (k_edge // 2) + group * 2 + jnp.where(late, 1, 0)
    at_inner = at - WB
    third = n_inner // 2
    to_inner = (at_inner // third) * (k_inner // 2) + group * third + at_inner % third
    permute = rows_are(piece, jnp.where((at < WB) | late, to_edge, k_edge + to_inner))

    for r in range(third, inner_msg.shape[1]):
        inner_msg[:, r, :] = jnp.zeros((n_row, 128), f32)
    for load in loads[:4]:
        load.wait()

    lane = lax.broadcasted_iota(jnp.int32, (st, bs), 1)
    for b in range(nb):
        block = jnp.where(
            lane < lens[b], psi_v[:, b * bs : (b + 1) * bs], jnp.zeros((), bf16)
        )
        own[b] = block
        if b < 2 * WB:
            low[WB + b] = block
        if b >= nb - 2 * WB:
            high[b - (nb - 2 * WB)] = block
    loads[4].wait()

    kept = lax.broadcasted_iota(jnp.int32, (n_row, st), 0) + col * n_row

    def product(b, blocks, base):
        top = blocks.shape[0] - 1
        chosen = [
            jnp.where(
                k < counts[b],
                blocks[jnp.clip(targets[k, b] - (row * nb + base), 0, top)],
                jnp.zeros((), bf16),
            )
            for k in range(kmax)
        ]
        total = lax.dot_general(
            jnp.concatenate([dip_v[b, k] for k in range(kmax)], axis=1),
            jnp.concatenate(chosen, axis=1),
            NT, preferred_element_type=f32,
        )
        return jnp.where(kept < lens[b], total, 0.0).astype(bf16).astype(f32)

    def send_pieces(part, msg, recv):
        for x, y in peers:
            to = x * 8 + y
            pltpu.make_async_remote_copy(
                src_ref=msg.at[to], dst_ref=recv.at[row],
                send_sem=a2a_send.at[part], recv_sem=a2a_recv.at[part],
                device_id=(to, col), device_id_type=MESH,
            ).start()
        recv[row] = msg[row]

    many = pl.ds(0, n_row - 1)

    def collect(part, recv, select):
        pltpu.make_async_copy(recv.at[many], recv.at[many], a2a_recv.at[part]).wait()
        rows = recv[...].reshape(-1, 128)
        if select is None:
            both = rows.T.astype(bf16)
        else:
            both = lax.dot_general(
                rows.astype(bf16), select, TN, preferred_element_type=f32
            ).astype(bf16)
        return jnp.concatenate([both[:st], both[st:]], axis=1)

    for r in range(third):
        inner_msg[:, r, :] = jnp.concatenate(
            [product(WB + r, own, 0), product(WB + third + r, own, 0)], axis=1
        )

    pl.semaphore_wait(barrier, n_row - 1 + n_col - 1)

    to_right = pltpu.make_async_remote_copy(
        src_ref=own.at[pl.ds(nb - WB, WB)], dst_ref=low.at[pl.ds(0, WB)],
        send_sem=halo_send.at[0], recv_sem=halo_recv.at[0],
        device_id=(lax.rem(row + 1, n_row), col), device_id_type=MESH,
    )
    to_left = pltpu.make_async_remote_copy(
        src_ref=own.at[pl.ds(0, WB)], dst_ref=high.at[pl.ds(2 * WB, WB)],
        send_sem=halo_send.at[1], recv_sem=halo_recv.at[1],
        device_id=(lax.rem(row + n_row - 1, n_row), col), device_id_type=MESH,
    )
    send_pieces(0, inner_msg, inner_recv)
    to_right.start()
    to_left.start()

    loads[5].wait()
    for c in range(n_col):
        span = slice(c * piece, (c + 1) * piece)
        eig_p[span, :] = jnp.dot(
            permute, eig_v[span, :], preferred_element_type=f32
        ).astype(bf16)

    to_right.wait_recv()
    to_left.wait_recv()
    edge_msg[:, 0, :] = jnp.concatenate([product(b, low, -WB) for b in range(WB)], axis=1)
    edge_msg[:, 1, :] = jnp.concatenate(
        [product(b, high, nb - 2 * WB) for b in range(nb - WB, nb)], axis=1
    )
    send_pieces(1, edge_msg, edge_recv)

    hops = [(s + 1) // 2 if s % 2 else n_col - s // 2 for s in range(1, n_col)]
    far_first = hops[::-1]
    turned = collect(0, inner_recv, select_inner)
    inner[col, 0:st, :] = turned[:, 0:128]
    inner[col, st : st + st // 2, :] = jnp.concatenate(
        [turned[: st // 2, 128:k_inner], turned[st // 2 :, 128:k_inner]], axis=1
    )
    for d in far_first:
        pltpu.make_async_remote_copy(
            src_ref=inner.at[col], dst_ref=inner.at[col],
            send_sem=z_send, recv_sem=z_recv.at[col],
            device_id=(row, lax.rem(col + d, n_col)), device_id_type=MESH,
        ).start()

    turned = collect(1, edge_recv, None)
    for h in range(HALVES):
        edge[h, col] = turned[h * half : (h + 1) * half, :]
        for d in far_first:
            pltpu.make_async_remote_copy(
                src_ref=edge.at[h, col], dst_ref=edge.at[h, col],
                send_sem=ze_send.at[h], recv_sem=ze_recv.at[h, col],
                device_id=(row, lax.rem(col + d, n_col)), device_id_type=MESH,
            ).start()

    for d in [0] + hops:
        c = lax.rem(col + n_col - d, n_col)
        if d:
            pltpu.make_async_copy(inner.at[c], inner.at[c], z_recv.at[c]).wait()
        tail = inner[c, st : st + st // 2, :]
        tail = jnp.concatenate([tail[:, 0:64], tail[:, 64:128]], axis=0)
        lhs = jnp.concatenate([inner[c, 0:st, :], tail], axis=1)
        base = pl.multiple_of(c * piece + k_edge, 64)
        part = jnp.dot(lhs, eig_p[pl.ds(base, k_inner), :], preferred_element_type=f32)
        acc[...] = acc[...] + part if d else part

    lanes = cols // 128
    tile = (
        pl.ds(pl.multiple_of((row // lanes) * 8, 8), 8),
        pl.ds(pl.multiple_of(lax.rem(row, lanes) * 128, 128), 128),
    )
    for h in range(HALVES):
        low_row = h * half
        for d in [0] + hops:
            c = lax.rem(col + n_col - d, n_col)
            if d:
                pltpu.make_async_copy(edge.at[h, c], edge.at[h, c], ze_recv.at[h, c]).wait()
            base = pl.multiple_of(c * piece, 64)
            acc[low_row : low_row + half, :] += jnp.dot(
                edge[h, c], eig_p[pl.ds(base, k_edge), :], preferred_element_type=f32
            )

        for x, y in peers:
            at_row = pl.multiple_of(low_row + x * 8, 8)
            at_lane = pl.multiple_of(y * 128, 128)
            pltpu.make_async_remote_copy(
                src_ref=acc.at[pl.ds(at_row, 8), pl.ds(at_lane, 128)],
                dst_ref=rs_recv.at[h, row],
                send_sem=rs_send.at[h], recv_sem=rs_sem.at[h],
                device_id=(x * 8 + y, col), device_id_type=MESH,
            ).start()
        rs_recv[h, row] = acc[
            pl.ds(pl.multiple_of(low_row + (row // lanes) * 8, 8), 8), tile[1]
        ]

    for h in range(HALVES):
        pltpu.make_async_copy(
            rs_recv.at[h, many], rs_recv.at[h, many], rs_sem.at[h]
        ).wait()
        mine = (pl.ds(pl.multiple_of(h * half + (row // lanes) * 8, 8), 8), tile[1])
        out_ref[mine] = jnp.sum(rs_recv[h], axis=0)

        for x, y in peers:
            pltpu.make_async_remote_copy(
                src_ref=out_ref.at[mine], dst_ref=out_ref.at[mine],
                send_sem=ag_send.at[h], recv_sem=ag_sem.at[h],
                device_id=(x * 8 + y, col), device_id_type=MESH,
            ).start()

    to_right.wait_send()
    to_left.wait_send()
    others = pl.ds(0, n_col - 1)
    pltpu.make_async_copy(inner.at[others], inner.at[others], z_send).wait()
    for h in range(HALVES):
        sent = (inner_msg, edge_msg)[h].at[many]
        pltpu.make_async_copy(sent, sent, a2a_send.at[h]).wait()
        pltpu.make_async_copy(edge.at[h, others], edge.at[h, others], ze_send.at[h]).wait()
        pltpu.make_async_copy(rs_recv.at[h, many], rs_recv.at[h, many], rs_send.at[h]).wait()
    for h in range(HALVES):
        pltpu.make_async_copy(rs_recv.at[h, many], rs_recv.at[h, many], ag_sem.at[h]).wait()
        pltpu.make_async_copy(rs_recv.at[h, many], rs_recv.at[h, many], ag_send.at[h]).wait()


def on_device(n_row, n_col, psi, block_len, targets, counts, dipole, eigvec):
    nb, kmax, _, bs = dipole.shape
    st = psi.shape[1]
    rows, cols = eigvec.shape
    n_edge, n_inner = 2 * WB, nb - 2 * WB
    bf16, f32, i32 = jnp.bfloat16, jnp.float32, jnp.int32
    dma = pltpu.SemaphoreType.DMA
    operands = [
        pltpu.with_memory_space_constraint(a, pltpu.HBM)
        for a in (block_len, targets.T, counts, psi.T, dipole, eigvec)
    ]
    turned = pl.pallas_call(
        functools.partial(body, n_row, n_col, nb, kmax, bs, st),
        out_shape=jax.ShapeDtypeStruct((st, cols), f32),
        in_specs=[pl.BlockSpec(memory_space=pltpu.HBM)] * 6,
        out_specs=pl.BlockSpec(memory_space=pltpu.VMEM),
        scratch_shapes=[
            pltpu.SMEM((nb,), i32),
            pltpu.SMEM((kmax, nb), i32),
            pltpu.SMEM((nb,), i32),
            pltpu.VMEM((st, nb * bs), bf16),
            pltpu.VMEM((nb, st, bs), bf16),
            pltpu.VMEM((3 * WB, st, bs), bf16),
            pltpu.VMEM((3 * WB, st, bs), bf16),
            pltpu.VMEM(dipole.shape, bf16),
            pltpu.VMEM((rows, cols), bf16),
            pltpu.VMEM((rows, cols), bf16),
            pltpu.VMEM((n_row, 4, 128), f32),
            pltpu.VMEM((n_row, 2, 128), f32),
            pltpu.VMEM((n_row, 4, 128), f32),
            pltpu.VMEM((n_row, 2, 128), f32),
            pltpu.VMEM((n_col, n_inner * n_row // 2, 128), bf16),
            pltpu.VMEM((HALVES, n_col, st // HALVES, n_edge * n_row), bf16),
            pltpu.VMEM((st, cols), f32),
            pltpu.VMEM((HALVES, n_row, 8, 128), f32),
            dma((6,)),
            dma((2,)),
            dma((2,)),
            dma((2,)),
            dma((2,)),
            dma,
            dma((n_col,)),
            dma((HALVES,)),
            dma((HALVES, n_col)),
            dma((HALVES,)),
            dma((HALVES,)),
            dma((HALVES,)),
            dma((HALVES,)),
        ],
        compiler_params=pltpu.CompilerParams(
            collective_id=0, has_side_effects=True, vmem_limit_bytes=24 * 2**20
        ),
    )(*operands)
    return turned.T


def solution(mesh):
    placed = (
        P("row", None),
        P("row"),
        P("row", None),
        P("row"),
        P("row", None, "col", None),
        P("row", "col"),
    )
    return jax.shard_map(
        functools.partial(on_device, mesh.shape["row"], mesh.shape["col"]),
        mesh=mesh, in_specs=placed, out_specs=P("col", None), check_vma=False,
    )
```

```python
import functools

import jax
import jax.numpy as jnp
from jax import lax
from jax.experimental import pallas as pl
from jax.experimental.pallas import tpu as pltpu
from jax.sharding import PartitionSpec as P

WB = 2
MESH = pl.DeviceIdType.MESH
NT = (((1,), (1,)), ((), ()))
TN = (((0,), (0,)), ((), ()))
HALVES = 2


def body(
    n_row, n_col, nb, kmax, bs, st,
    lens_hbm, targets_hbm, counts_hbm, psi_hbm, dip_hbm, eig_hbm, out_ref,
    lens, targets, counts, psi_v, own, low, high, dip_v, eig_v, eig_p,
    inner_msg, edge_msg, inner_recv, edge_recv, inner, edge, acc, rs_recv,
    ld_sem, halo_send, halo_recv, a2a_send, a2a_recv, z_send, z_recv, ze_send, ze_recv,
    rs_send, rs_sem, ag_send, ag_sem,
):
    row = lax.axis_index("row")
    col = lax.axis_index("col")
    f32, bf16 = jnp.float32, jnp.bfloat16
    n_edge = 2 * WB
    n_inner = nb - n_edge
    piece = nb * n_row
    k_edge = n_edge * n_row
    k_inner = n_inner * n_row
    cols = eig_v.shape[1]
    half = st // HALVES

    loads = [
        pltpu.make_async_copy(src, dst, ld_sem.at[i])
        for i, (src, dst) in enumerate(
            [
                (lens_hbm, lens),
                (targets_hbm, targets),
                (counts_hbm, counts),
                (psi_hbm, psi_v),
                (dip_hbm, dip_v),
                (eig_hbm, eig_v),
            ]
        )
    ]

    chip_x, chip_y, core = row // 8, lax.rem(row // 2, 4), lax.rem(row, 2)
    at_x = [lax.rem(chip_x + d, 4) for d in range(4)]
    at_y = [[lax.rem(chip_y + d, 4) * 2 + c for c in (core, 1 - core)] for d in range(4)]
    offsets = [(x, y, c) for x in range(4) for y in range(4) for c in range(2)][1:]
    offsets.sort(key=lambda o: (-(min(o[0], 4 - o[0]) + min(o[1], 4 - o[1])), o[2], (o[0] * 3 + o[1] * 5) % 7))
    peers = [(at_x[x], at_y[y][c]) for x, y, c in offsets]

    barrier = pltpu.get_barrier_semaphore()

    for x, y in peers:
        pl.semaphore_signal(
            barrier, inc=1, device_id=(x * 8 + y, col), device_id_type=MESH
        )
    for i in range(1, n_col):
        pl.semaphore_signal(
            barrier, inc=1, device_id=(row, lax.rem(col + i, n_col)), device_id_type=MESH
        )
    for load in loads:
        load.start()

    def rows_are(count, wanted):
        held = lax.broadcasted_iota(jnp.int32, (count, wanted.shape[1]), 0)
        return jnp.where(held == wanted, 1.0, 0.0).astype(bf16)

    def kept_rows(used, held):
        at = lax.broadcasted_iota(jnp.int32, (1, used * n_row), 1)
        return rows_are(held * n_row, at + (held - used) * (at // used))

    select_inner = kept_rows(n_inner // 2, inner_msg.shape[1])
    at = lax.broadcasted_iota(jnp.int32, (1, piece), 1)
    group, at = at // nb, at % nb
    late = at >= nb - WB
    at_edge = jnp.where(late, at - (nb - WB), at)
    to_edge = at_edge * (k_edge // 2) + group * 2 + jnp.where(late, 1, 0)
    at_inner = at - WB
    third = n_inner // 2
    to_inner = (at_inner // third) * (k_inner // 2) + group * third + at_inner % third
    permute = rows_are(piece, jnp.where((at < WB) | late, to_edge, k_edge + to_inner))

    for r in range(third, inner_msg.shape[1]):
        inner_msg[:, r, :] = jnp.zeros((n_row, 128), f32)
    for load in loads[:4]:
        load.wait()

    lane = lax.broadcasted_iota(jnp.int32, (st, bs), 1)
    for b in range(nb):
        block = jnp.where(
            lane < lens[b], psi_v[:, b * bs : (b + 1) * bs], jnp.zeros((), bf16)
        )
        own[b] = block
        if b < 2 * WB:
            low[WB + b] = block
        if b >= nb - 2 * WB:
            high[b - (nb - 2 * WB)] = block
    loads[4].wait()

    kept = lax.broadcasted_iota(jnp.int32, (n_row, st), 0) + col * n_row

    def product(b, blocks, base):
        top = blocks.shape[0] - 1
        chosen = [
            jnp.where(
                k < counts[b],
                blocks[jnp.clip(targets[k, b] - (row * nb + base), 0, top)],
                jnp.zeros((), bf16),
            )
            for k in range(kmax)
        ]
        total = lax.dot_general(
            jnp.concatenate([dip_v[b, k] for k in range(kmax)], axis=1),
            jnp.concatenate(chosen, axis=1),
            NT, preferred_element_type=f32,
        )
        return jnp.where(kept < lens[b], total, 0.0).astype(bf16).astype(f32)

    def send_pieces(part, msg, recv):
        for x, y in peers:
            to = x * 8 + y
            pltpu.make_async_remote_copy(
                src_ref=msg.at[to], dst_ref=recv.at[row],
                send_sem=a2a_send.at[part], recv_sem=a2a_recv.at[part],
                device_id=(to, col), device_id_type=MESH,
            ).start()
        recv[row] = msg[row]

    many = pl.ds(0, n_row - 1)

    def collect(part, recv, select):
        pltpu.make_async_copy(recv.at[many], recv.at[many], a2a_recv.at[part]).wait()
        rows = recv[...].reshape(-1, 128)
        if select is None:
            both = rows.T.astype(bf16)
        else:
            both = lax.dot_general(
                rows.astype(bf16), select, TN, preferred_element_type=f32
            ).astype(bf16)
        return jnp.concatenate([both[:st], both[st:]], axis=1)

    for r in range(third):
        inner_msg[:, r, :] = jnp.concatenate(
            [product(WB + r, own, 0), product(WB + third + r, own, 0)], axis=1
        )

    pl.semaphore_wait(barrier, n_row - 1 + n_col - 1)

    to_right = pltpu.make_async_remote_copy(
        src_ref=own.at[pl.ds(nb - WB, WB)], dst_ref=low.at[pl.ds(0, WB)],
        send_sem=halo_send.at[0], recv_sem=halo_recv.at[0],
        device_id=(lax.rem(row + 1, n_row), col), device_id_type=MESH,
    )
    to_left = pltpu.make_async_remote_copy(
        src_ref=own.at[pl.ds(0, WB)], dst_ref=high.at[pl.ds(2 * WB, WB)],
        send_sem=halo_send.at[1], recv_sem=halo_recv.at[1],
        device_id=(lax.rem(row + n_row - 1, n_row), col), device_id_type=MESH,
    )
    send_pieces(0, inner_msg, inner_recv)
    to_right.start()
    to_left.start()

    loads[5].wait()
    for c in range(n_col):
        span = slice(c * piece, (c + 1) * piece)
        eig_p[span, :] = jnp.dot(
            permute, eig_v[span, :], preferred_element_type=f32
        ).astype(bf16)

    to_right.wait_recv()
    to_left.wait_recv()
    edge_msg[:, 0, :] = jnp.concatenate([product(b, low, -WB) for b in range(WB)], axis=1)
    edge_msg[:, 1, :] = jnp.concatenate(
        [product(b, high, nb - 2 * WB) for b in range(nb - WB, nb)], axis=1
    )
    send_pieces(1, edge_msg, edge_recv)

    hops = [(s + 1) // 2 if s % 2 else n_col - s // 2 for s in range(1, n_col)]
    far_first = hops[::-1]
    turned = collect(0, inner_recv, select_inner)
    inner[col, 0:st, :] = turned[:, 0:128]
    inner[col, st : st + st // 2, :] = jnp.concatenate(
        [turned[: st // 2, 128:k_inner], turned[st // 2 :, 128:k_inner]], axis=1
    )
    for d in far_first:
        pltpu.make_async_remote_copy(
            src_ref=inner.at[col], dst_ref=inner.at[col],
            send_sem=z_send, recv_sem=z_recv.at[col],
            device_id=(row, lax.rem(col + d, n_col)), device_id_type=MESH,
        ).start()

    turned = collect(1, edge_recv, None)
    for h in range(HALVES):
        edge[h, col] = turned[h * half : (h + 1) * half, :]
        for d in far_first:
            pltpu.make_async_remote_copy(
                src_ref=edge.at[h, col], dst_ref=edge.at[h, col],
                send_sem=ze_send.at[h], recv_sem=ze_recv.at[h, col],
                device_id=(row, lax.rem(col + d, n_col)), device_id_type=MESH,
            ).start()

    for d in [0] + hops:
        c = lax.rem(col + n_col - d, n_col)
        if d:
            pltpu.make_async_copy(inner.at[c], inner.at[c], z_recv.at[c]).wait()
        tail = inner[c, st : st + st // 2, :]
        tail = jnp.concatenate([tail[:, 0:64], tail[:, 64:128]], axis=0)
        lhs = jnp.concatenate([inner[c, 0:st, :], tail], axis=1)
        base = pl.multiple_of(c * piece + k_edge, 64)
        part = jnp.dot(lhs, eig_p[pl.ds(base, k_inner), :], preferred_element_type=f32)
        acc[...] = acc[...] + part if d else part

    lanes = cols // 128
    tile = (
        pl.ds(pl.multiple_of((row // lanes) * 8, 8), 8),
        pl.ds(pl.multiple_of(lax.rem(row, lanes) * 128, 128), 128),
    )
    for h in range(HALVES):
        low_row = h * half
        for d in [0] + hops:
            c = lax.rem(col + n_col - d, n_col)
            if d:
                pltpu.make_async_copy(edge.at[h, c], edge.at[h, c], ze_recv.at[h, c]).wait()
            base = pl.multiple_of(c * piece, 64)
            acc[low_row : low_row + half, :] += jnp.dot(
                edge[h, c], eig_p[pl.ds(base, k_edge), :], preferred_element_type=f32
            )

        for x, y in peers:
            at_row = pl.multiple_of(low_row + x * 8, 8)
            at_lane = pl.multiple_of(y * 128, 128)
            pltpu.make_async_remote_copy(
                src_ref=acc.at[pl.ds(at_row, 8), pl.ds(at_lane, 128)],
                dst_ref=rs_recv.at[h, row],
                send_sem=rs_send.at[h], recv_sem=rs_sem.at[h],
                device_id=(x * 8 + y, col), device_id_type=MESH,
            ).start()
        rs_recv[h, row] = acc[
            pl.ds(pl.multiple_of(low_row + (row // lanes) * 8, 8), 8), tile[1]
        ]

    for h in range(HALVES):
        pltpu.make_async_copy(
            rs_recv.at[h, many], rs_recv.at[h, many], rs_sem.at[h]
        ).wait()
        mine = (pl.ds(pl.multiple_of(h * half + (row // lanes) * 8, 8), 8), tile[1])
        out_ref[mine] = jnp.sum(rs_recv[h], axis=0)

        for x, y in peers:
            pltpu.make_async_remote_copy(
                src_ref=out_ref.at[mine], dst_ref=out_ref.at[mine],
                send_sem=ag_send.at[h], recv_sem=ag_sem.at[h],
                device_id=(x * 8 + y, col), device_id_type=MESH,
            ).start()

    to_right.wait_send()
    to_left.wait_send()
    others = pl.ds(0, n_col - 1)
    pltpu.make_async_copy(inner.at[others], inner.at[others], z_send).wait()
    for h in range(HALVES):
        sent = (inner_msg, edge_msg)[h].at[many]
        pltpu.make_async_copy(sent, sent, a2a_send.at[h]).wait()
        pltpu.make_async_copy(edge.at[h, others], edge.at[h, others], ze_send.at[h]).wait()
        pltpu.make_async_copy(rs_recv.at[h, many], rs_recv.at[h, many], rs_send.at[h]).wait()
    for h in range(HALVES):
        pltpu.make_async_copy(rs_recv.at[h, many], rs_recv.at[h, many], ag_sem.at[h]).wait()
        pltpu.make_async_copy(rs_recv.at[h, many], rs_recv.at[h, many], ag_send.at[h]).wait()


def on_device(n_row, n_col, psi, block_len, targets, counts, dipole, eigvec):
    nb, kmax, _, bs = dipole.shape
    st = psi.shape[1]
    rows, cols = eigvec.shape
    n_edge, n_inner = 2 * WB, nb - 2 * WB
    bf16, f32, i32 = jnp.bfloat16, jnp.float32, jnp.int32
    dma = pltpu.SemaphoreType.DMA
    operands = [
        pltpu.with_memory_space_constraint(a, pltpu.HBM)
        for a in (block_len, targets.T, counts, psi.T, dipole, eigvec)
    ]
    turned = pl.pallas_call(
        functools.partial(body, n_row, n_col, nb, kmax, bs, st),
        out_shape=jax.ShapeDtypeStruct((st, cols), f32),
        in_specs=[pl.BlockSpec(memory_space=pltpu.HBM)] * 6,
        out_specs=pl.BlockSpec(memory_space=pltpu.VMEM),
        scratch_shapes=[
            pltpu.SMEM((nb,), i32),
            pltpu.SMEM((kmax, nb), i32),
            pltpu.SMEM((nb,), i32),
            pltpu.VMEM((st, nb * bs), bf16),
            pltpu.VMEM((nb, st, bs), bf16),
            pltpu.VMEM((3 * WB, st, bs), bf16),
            pltpu.VMEM((3 * WB, st, bs), bf16),
            pltpu.VMEM(dipole.shape, bf16),
            pltpu.VMEM((rows, cols), bf16),
            pltpu.VMEM((rows, cols), bf16),
            pltpu.VMEM((n_row, 4, 128), f32),
            pltpu.VMEM((n_row, 2, 128), f32),
            pltpu.VMEM((n_row, 4, 128), f32),
            pltpu.VMEM((n_row, 2, 128), f32),
            pltpu.VMEM((n_col, n_inner * n_row // 2, 128), bf16),
            pltpu.VMEM((HALVES, n_col, st // HALVES, n_edge * n_row), bf16),
            pltpu.VMEM((st, cols), f32),
            pltpu.VMEM((HALVES, n_row, 8, 128), f32),
            dma((6,)),
            dma((2,)),
            dma((2,)),
            dma((2,)),
            dma((2,)),
            dma,
            dma((n_col,)),
            dma((HALVES,)),
            dma((HALVES, n_col)),
            dma((HALVES,)),
            dma((HALVES,)),
            dma((HALVES,)),
            dma((HALVES,)),
        ],
        compiler_params=pltpu.CompilerParams(
            collective_id=0, has_side_effects=True, vmem_limit_bytes=24 * 2**20
        ),
    )(*operands)
    return turned.T


def solution(mesh):
    placed = (
        P("row", None),
        P("row"),
        P("row", None),
        P("row"),
        P("row", None, "col", None),
        P("row", "col"),
    )
    return jax.shard_map(
        functools.partial(on_device, mesh.shape["row"], mesh.shape["col"]),
        mesh=mesh, in_specs=placed, out_specs=P("col", None), check_vma=False,
    )
```
